256 devices in a mesh: row: 2 (over x_hi), col: 64 (over z, y, core), sk: 2 (over x_lo).
Axes of the slice: x: 4 (x_hi: 2, x_lo: 2; x = x_hi * 2 + x_lo), y: 4, z: 8, core: 2. Of those that a mesh axis runs over, the one named last changes fastest.
Arguments:
- tiles: bfloat16 [2, 64, 4, 1024, 1024], P('row', 'col'), may hold values from -0.09375 to 0.09375
- tile_rows: int32 [2, 64, 4], P('row', 'col'), may hold values from 0 to 1, as said below
- tile_cols: int32 [2, 64, 4], P('row', 'col'), may hold values from 0 to 1, as said below
- tile_count: int32 [2, 64], P('row', 'col'), may hold values from 1 to 4, as said below
- sketch: bfloat16 [131072, 512], P('col', 'sk'), may hold values from -6 to 6
Outputs:
- basis: float32 [131072, 512], P('col', 'sk')
- factor: float32 [512, 512], replicated
The draws below stay inside these ranges and needn't reach their ends.
Inputs may be any that keep to these rules, and one draw needn't show every extreme that they name: `tile_rows`: within one pair of slabs the slots name distinct (row, column) tile positions. `tile_cols`: within one pair of slabs the slots name distinct (row, column) tile positions. `tile_count`: some pair of slabs has all 4 slots live.
All inputs are finite; a program needn't handle non-finite values.
Results may differ from the reference program's by a relative error of at most 0.0031.
Values sent between devices are 32-bit elements; how exact they have to be, the bound alone decides.
No kernel may reach another device: no remote copies, remote signals or barrier semaphores. Data moves between devices by JAX's collectives and lax.ppermute only.
A program may use at most 64 MiB of HBM per device.

```python
import jax
import jax.numpy as jnp
from jax import lax

TB = 1024
K = 512
RB = 2
CB = 2
SLOTS = 4
N = 131072
N_ROW = 2
N_COL = 64


def tile_slots(key):
    places = RB * CB
    scores = jax.random.randint(key, (N_ROW, N_COL, places), 0, 1 << 20) * places + jnp.arange(places, dtype=jnp.int32)
    return jnp.argsort(scores, axis=-1)[..., :SLOTS].astype(jnp.int32)


def draw_tile_rows(key, part):
    return tile_slots(key) // CB


def draw_tile_cols(key, part):
    return tile_slots(key) % CB


def draw_tile_count(key, part):
    key = jax.random.fold_in(key, 7)
    first, second = jax.random.split(key)
    counts = jax.random.randint(first, (N_ROW * N_COL,), 1, SLOTS + 1)
    chosen = jax.random.randint(second, (), 0, N_ROW * N_COL)
    counts = jnp.where(jnp.arange(N_ROW * N_COL) == chosen, SLOTS, counts)
    return counts.reshape(N_ROW, N_COL).astype(jnp.int32)


def block_levels(rng, extent, pieces, low, top_value):
    factor_of = 1.0
    for position, parts in pieces:
        heights = jax.random.uniform(jax.random.fold_in(jax.random.fold_in(rng, 6), position), (parts,), jnp.float32, low / len(pieces), top_value / len(pieces))
        factor_of = factor_of * jnp.repeat(jnp.exp(heights), extent[position] // parts).reshape((-1,) + (1,) * (len(extent) - 1 - position))
    return factor_of


def scatter_about(key, dims, spread, most, cuts=(), kind=jnp.bfloat16):
    values = spread * jax.random.normal(key, dims, jnp.float32)
    if cuts:
        values = values * block_levels(key, dims, cuts, -0.22, 0.18)
    return jnp.clip(values, -most, most).astype(kind)


def setup_inputs(seed: int = 0) -> dict:
    splits = jax.random.split(jax.random.key(seed), 6)
    tiles = scatter_about(splits[0], (N_ROW, N_COL, SLOTS, TB, TB), (TB * 4) ** -0.5, 0.09375, ((0, 2), (1, 64)))
    tile_rows = draw_tile_rows(jax.random.fold_in(splits[5], 71), 0)
    tile_cols = draw_tile_cols(jax.random.fold_in(splits[5], 71), 0)
    tile_count = draw_tile_count(jax.random.fold_in(splits[5], 71), 0)
    sketch = scatter_about(splits[4], (N, K), 1.0, 6.0, ((0, 64), (1, 2)))
    return {"tiles": tiles, "tile_rows": tile_rows, "tile_cols": tile_cols, "tile_count": tile_count, "sketch": sketch}


def reference(tiles, tile_rows, tile_cols, tile_count, sketch):
    nrow, ncol, slots, tb, _ = tiles.shape
    width = sketch.shape[1]
    high = lax.Precision.HIGHEST
    sketch_blocks = sketch.reshape(ncol, CB, tb, width)
    live = (jnp.arange(slots)[None, None, :] < tile_count[:, :, None]).astype(jnp.float32)
    row_weights = (tile_rows[..., None] == jnp.arange(RB)[None, None, None, :]).astype(jnp.float32) * live[..., None]
    col_weights = (tile_cols[..., None] == jnp.arange(CB)[None, None, None, :]).astype(jnp.float32) * live[..., None]

    def row_slab(args):
        blocks, cols, weights = args
        picked = sketch_blocks[jnp.arange(ncol)[:, None], cols]
        prod = jnp.einsum('csij,csjk->csik', blocks.astype(jnp.float32), picked.astype(jnp.float32), precision=high)
        return jnp.einsum('csr,csik->rik', weights, prod, precision=high)
    slab_y = (lax.map(row_slab, (tiles, tile_cols, row_weights)) * 0.75).astype(jnp.bfloat16)

    def col_slab(args):
        blocks, rows, weights = args
        picked = slab_y[jnp.arange(nrow)[:, None], rows]
        prod = jnp.einsum('rsji,rsjk->rsik', blocks.astype(jnp.float32), picked.astype(jnp.float32), precision=high)
        return jnp.einsum('rsb,rsik->bik', weights, prod, precision=high)
    slab_z = lax.map(col_slab, (jnp.swapaxes(tiles, 0, 1), jnp.swapaxes(tile_rows, 0, 1), jnp.swapaxes(col_weights, 0, 1)))
    whole_z = slab_z.reshape(ncol * CB * tb, width)
    gram = jnp.dot(whole_z.T.astype(jnp.float32), whole_z.astype(jnp.float32), precision=high, preferred_element_type=jnp.float32) / whole_z.shape[0]
    lower = jnp.linalg.cholesky(gram)
    inverse = jax.scipy.linalg.solve_triangular(lower, jnp.eye(width, dtype=jnp.float32), lower=True)
    basis = jnp.dot(whole_z.astype(jnp.float32), inverse.T.astype(jnp.float32), precision=high, preferred_element_type=jnp.float32)
    return (basis, lower.T)
```

```python
import functools

import jax
import jax.numpy as jnp
from jax import lax
from jax.experimental import pallas as pl
from jax.experimental.pallas import tpu as pltpu
from jax.sharding import Mesh, PartitionSpec as P

HIGH = lax.Precision.HIGHEST
F32 = jnp.float32
BF16 = jnp.bfloat16
PLANE = ("z", "y")
RING = ("row", "sk")
SHEET = ("row", "y", "sk")
LIMIT = 48 * 1024 * 1024
SIDE = 128
GROUP = 8
SUB = 32


def dot(a, b, dims, precision=None):
    return lax.dot_general(a, b, (dims, ((), ())), precision=precision, preferred_element_type=F32)


def tile_spec(tb, parts):
    def place(s, i, rows, cols, count):
        live = s < count[0]
        return (jnp.where(live, s, count[0] - 1), jnp.where(live, i, parts - 1), 0)

    return pl.BlockSpec((None, tb // parts, tb), place)


def forward_kernel(parts, rows, cols, count, tiles, sketch, keep, send):
    s = pl.program_id(0)
    i = pl.program_id(1)
    core = lax.axis_index("core")
    depth = tiles.shape[0]

    @pl.when((s == 0) & (i == 0))
    def _():
        keep[...] = jnp.zeros_like(keep)
        send[...] = jnp.zeros_like(send)

    @pl.when(s < count[0])
    def _():
        prod = dot(tiles[...], sketch[cols[s]], ((1,), (0,)))
        here = pl.ds(pl.multiple_of(i * depth, depth), depth)

        @pl.when(rows[s] == core)
        def _():
            keep[here, :] += prod

        @pl.when(rows[s] != core)
        def _():
            send[here, :] += prod


def forward(rows, cols, count, tiles, sketch):
    slots, tb, _ = tiles.shape
    width = sketch.shape[-1]
    parts = 2
    half = jax.ShapeDtypeStruct((tb, width), F32)
    whole = pl.BlockSpec((tb, width), lambda s, i, *_: (0, 0))
    return pl.pallas_call(
        functools.partial(forward_kernel, parts),
        grid_spec=pltpu.PrefetchScalarGridSpec(
            num_scalar_prefetch=3,
            grid=(slots, parts),
            in_specs=[tile_spec(tb, parts), pl.BlockSpec(sketch.shape, lambda s, i, *_: (0, 0, 0))],
            out_specs=[whole, whole],
        ),
        out_shape=[half, half],
        compiler_params=pltpu.CompilerParams(vmem_limit_bytes=LIMIT),
        name="forward",
    )(rows, cols, count, tiles, sketch)


def backward_kernel(parts, rows, cols, count, tiles, own, other, out, flat):
    s = pl.program_id(0)
    i = pl.program_id(1)
    core = lax.axis_index("core")
    depth, tb = tiles.shape

    @pl.when((s == 0) & (i == 0))
    def _():
        out[...] = jnp.zeros_like(out)
        for p in range(parts):
            flat[core, p] = own[p * depth : (p + 1) * depth, :].astype(BF16).T
            flat[1 - core, p] = other[p * depth : (p + 1) * depth, :].astype(BF16).T

    @pl.when(s < count[0])
    def _():
        prod = dot(flat[rows[s], i], tiles[...], ((1,), (0,)))
        half = tb // 2
        for q in range(2):
            out[2 * cols[s] + q] += prod[:, q * half : (q + 1) * half]


def backward(rows, cols, count, tiles, own, other):
    slots, tb, _ = tiles.shape
    width = own.shape[-1]
    parts = 2
    whole = pl.BlockSpec((tb, width), lambda s, i, *_: (0, 0))
    shape = (4, width, tb // 2)
    return pl.pallas_call(
        functools.partial(backward_kernel, parts),
        grid_spec=pltpu.PrefetchScalarGridSpec(
            num_scalar_prefetch=3,
            grid=(slots, parts),
            in_specs=[tile_spec(tb, parts), whole, whole],
            out_specs=pl.BlockSpec(shape, lambda s, i, *_: (0, 0, 0)),
            scratch_shapes=[pltpu.VMEM((2, parts, width, tb // parts), BF16)],
        ),
        out_shape=jax.ShapeDtypeStruct(shape, F32),
        compiler_params=pltpu.CompilerParams(vmem_limit_bytes=LIMIT),
        name="backward",
    )(rows, cols, count, tiles, own, other)


def block_pairs(n):
    return [(i, j) for i in range(n) for j in range(i, n)]


def gram_kernel(parts, zt, keep, send):
    core = lax.axis_index("core")
    narrow = parts.shape[1]
    zt[0:narrow, :] = parts[0] + parts[2]
    zt[narrow:, :] = parts[1] + parts[3]
    width = zt.shape[0]
    pairs = block_pairs(width // SIDE)
    half = len(pairs) // 2
    for i in range(width // SIDE):
        lhs = zt[i * SIDE : (i + 1) * SIDE, :]
        prod = dot(lhs, zt[i * SIDE :, :], ((1,), (1,)), HIGH)
        for n, (a, b) in enumerate(pairs):
            if a != i:
                continue
            block = prod[:, (b - i) * SIDE : (b - i + 1) * SIDE]

            @pl.when(core == n // half)
            def _():
                keep[n % half] = block

            @pl.when(core != n // half)
            def _():
                send[n % half] = block


def gram_of(parts):
    _, narrow, chunk = parts.shape
    width = 2 * narrow
    half = len(block_pairs(width // SIDE)) // 2
    blocks = jax.ShapeDtypeStruct((half, SIDE, SIDE), F32)
    return pl.pallas_call(
        gram_kernel,
        out_shape=[jax.ShapeDtypeStruct((width, chunk), F32), blocks, blocks],
        compiler_params=pltpu.CompilerParams(vmem_limit_bytes=LIMIT),
        name="gram",
    )(parts)


def eliminate(d, base):
    count = SUB // GROUP
    lanes = d.shape[1] // SIDE
    sub = lax.broadcasted_iota(jnp.int32, (GROUP, SIDE), 0)
    rows = [
        [d[base + GROUP * p : base + GROUP * (p + 1), SIDE * t : SIDE * (t + 1)] for t in range(lanes)]
        for p in range(count)
    ]
    for b in range(count):
        first = base + GROUP * b
        cols = [
            [jnp.broadcast_to(rows[p][0][:, first + m : first + m + 1], (GROUP, SIDE)) for p in range(b, count)]
            for m in range(GROUP)
        ]
        scale = jnp.zeros((GROUP, SIDE), F32)
        for m in range(GROUP):
            pivot = jnp.broadcast_to(cols[m][0][m : m + 1, :], (GROUP, SIDE))
            inv = lax.rsqrt(pivot)
            scale = jnp.where(sub == m, inv, scale)
            low = [c * inv for c in cols[m]]
            low[0] = jnp.where(sub > m, low[0], 0.0)
            for n in range(m + 1, GROUP):
                mult = jnp.broadcast_to(low[0][n : n + 1, :], (GROUP, SIDE))
                cols[n] = [c - l * mult for c, l in zip(cols[n], low)]
            for t in range(lanes):
                u = jnp.broadcast_to(rows[b][t][m : m + 1, :], (GROUP, SIDE)) * inv
                for p in range(b, count):
                    rows[p][t] = rows[p][t] - low[p - b] * u
        for t in range(lanes):
            rows[b][t] = rows[b][t] * scale
    for p in range(count):
        for t in range(lanes):
            d[base + GROUP * p : base + GROUP * (p + 1), SIDE * t : SIDE * (t + 1)] = rows[p][t]


def cholesky_kernel(scale, own, other, upper, inverse, d):
    core = lax.axis_index("core")
    width = upper.shape[0]
    nb = width // SIDE
    pairs = block_pairs(nb)
    half = len(pairs) // 2
    upper[...] = jnp.zeros_like(upper)
    inverse[...] = jnp.zeros_like(inverse)
    for n, (i, j) in enumerate(pairs):
        spot = (slice(i * SIDE, (i + 1) * SIDE), slice(j * SIDE, (j + 1) * SIDE))

        @pl.when(core == n // half)
        def _():
            upper[spot] = own[n % half] * scale

        @pl.when(core != n // half)
        def _():
            upper[spot] = other[n % half] * scale

    row = lax.broadcasted_iota(jnp.int32, (SIDE, SIDE), 0)
    col = lax.broadcasted_iota(jnp.int32, (SIDE, SIDE), 1)
    eye = (row == col).astype(F32)

    def step(k, carry):
        here = pl.ds(pl.multiple_of(k * SIDE, SIDE), SIDE)
        d[:, 0:SIDE] = upper[here, here]
        d[:, SIDE:] = eye
        for s in range(SIDE // SUB):
            base = s * SUB
            eliminate(d, base)
            if base + SUB < SIDE:
                panel = d[base : base + SUB, :]
                left = panel[:, base + SUB : SIDE]
                d[base + SUB :, :] -= dot(left, panel, ((0,), (0,)), HIGH)
        upper[here, here] = jnp.where(row <= col, d[:, 0:SIDE], 0.0)
        inverse[here, here] = jnp.where(row >= col, d[:, SIDE:], 0.0)

        for kk in range(nb):

            @pl.when(k == kk)
            def _():
                lo, hi = kk * SIDE, (kk + 1) * SIDE
                w = inverse[lo:hi, lo:hi]
                if hi < width:
                    upper[lo:hi, hi:] = dot(w, upper[lo:hi, hi:], ((1,), (0,)), HIGH)
                if lo > 0:
                    inverse[lo:hi, 0:lo] = dot(w, inverse[lo:hi, 0:lo], ((1,), (0,)), HIGH)
                if hi < width:
                    left = upper[lo:hi, hi:].T
                    prod = dot(left, upper[lo:hi, hi:], ((1,), (0,)), HIGH)
                    for i in range(kk + 1, nb):
                        r = slice(i * SIDE, (i + 1) * SIDE)
                        o = slice((i - kk - 1) * SIDE, (i - kk) * SIDE)
                        upper[r, i * SIDE :] -= prod[o, (i - kk - 1) * SIDE :]
                    inverse[hi:, 0:hi] -= dot(left, inverse[lo:hi, 0:hi], ((1,), (0,)), HIGH)

        return carry

    lax.fori_loop(0, nb, step, 0)


def cholesky(own, other, total_rows, width):
    square = jax.ShapeDtypeStruct((width, width), F32)
    return pl.pallas_call(
        functools.partial(cholesky_kernel, 1.0 / total_rows),
        out_shape=[square, square],
        scratch_shapes=[pltpu.VMEM((SIDE, 2 * SIDE), F32)],
        compiler_params=pltpu.CompilerParams(vmem_limit_bytes=LIMIT),
        name="cholesky",
    )(own, other)


def basis_kernel(sk, inverse, zt, out):
    out[...] = dot(inverse[...], zt[...], ((1,), (0,)), HIGH).T


def basis_of(inverse, zts, sk):
    width = inverse.shape[0]
    narrow = width // 2
    quarters, _, chunk = zts.shape
    return pl.pallas_call(
        basis_kernel,
        grid_spec=pltpu.PrefetchScalarGridSpec(
            num_scalar_prefetch=1,
            grid=(quarters,),
            in_specs=[
                pl.BlockSpec((narrow, width), lambda q, sk: (sk[0], 0)),
                pl.BlockSpec((None, width, chunk), lambda q, sk: (q, 0, 0)),
            ],
            out_specs=pl.BlockSpec((chunk, narrow), lambda q, sk: (q, 0)),
        ),
        out_shape=jax.ShapeDtypeStruct((quarters * chunk, narrow), F32),
        compiler_params=pltpu.CompilerParams(vmem_limit_bytes=LIMIT),
        name="basis",
    )(sk, inverse, zts)


def swap(x):
    return lax.ppermute(x, "core", [(0, 1), (1, 0)])


def exchange(x, axes):
    return lax.all_to_all(x, axes, 0, 0, tiled=True)


def spread(x, axes):
    n = lax.axis_size(axes)
    return exchange(jnp.broadcast_to(x[None], (n,) + x.shape), axes)


def on_device(tiles, tile_rows, tile_cols, tile_count, sketch):
    blocks = tiles[0, 0]
    rows = tile_rows[0, 0]
    cols = tile_cols[0, 0]
    count = tile_count[0]
    tb = blocks.shape[1]
    narrow = sketch.shape[1]
    width = narrow * lax.axis_size("sk")
    total_rows = sketch.shape[0] * lax.axis_size(("z", "y", "core"))

    keep, send = forward(rows, cols, count, blocks, sketch.reshape(-1, tb, narrow))
    half = keep + swap(send)
    plane = lax.axis_size(PLANE)
    pieces = exchange(half.reshape(plane, tb // plane, narrow), PLANE)
    piece = jnp.sum(pieces, axis=0) * 0.75
    own_y = spread(piece, PLANE).reshape(tb, narrow)
    other_y = swap(own_y)

    quarters = backward(rows, cols, count, blocks, own_y, other_y)
    zt, keep, send = gram_of(exchange(quarters, RING))
    zts = lax.all_gather(zt, RING, axis=0)

    half = keep + swap(send)
    sheet = lax.axis_size(SHEET)
    pieces = exchange(half.reshape(sheet, -1, SIDE), SHEET)
    piece = jnp.sum(pieces, axis=0)
    piece = jnp.sum(spread(piece, "z"), axis=0)
    own_g = spread(piece, SHEET).reshape(keep.shape)
    other_g = swap(own_g)

    upper, inverse = cholesky(own_g, other_g, total_rows, width)
    sk = lax.axis_index("sk").astype(jnp.int32).reshape(1)
    return basis_of(inverse, zts, sk), upper


def solution(mesh):
    fine = Mesh(mesh.devices.reshape(2, 8, 4, 2, 2), ("row", "z", "y", "core", "sk"))
    col = ("z", "y", "core")
    return jax.shard_map(
        on_device,
        mesh=fine,
        in_specs=(
            P("row", col, None, None, None),
            P("row", col, None),
            P("row", col, None),
            P("row", col),
            P(col, "sk"),
        ),
        out_specs=(P(col, "sk"), P()),
        check_vma=False,
    )
```

```python
import functools

import jax
import jax.numpy as jnp
from jax import lax
from jax.experimental import pallas as pl
from jax.experimental.pallas import tpu as pltpu
from jax.sharding import Mesh, PartitionSpec as P

HIGH = lax.Precision.HIGHEST
F32 = jnp.float32
BF16 = jnp.bfloat16
RING = ("row", "sk")
SHEET = ("row", "y", "sk")
LIMIT = 48 * 1024 * 1024
SIDE = 128
GROUP = 8
SUB = 32


def dot(a, b, dims, precision=None):
    return lax.dot_general(a, b, (dims, ((), ())), precision=precision, preferred_element_type=F32)


PARTS = 4


def fetch(tiles, held, sems):
    slots, tb, _ = tiles.shape
    depth = tb // PARTS
    copies = [
        [
            pltpu.make_async_copy(
                tiles.at[s, pl.ds(p * depth, depth)], held.at[s, pl.ds(p * depth, depth)], sems.at[s, p]
            )
            for p in range(PARTS)
        ]
        for s in range(slots)
    ]
    for slot in copies[:2]:
        for copy in slot:
            copy.start()
    return copies


def await_tile(copies, s):
    for copy in copies[s]:
        copy.wait()
    for copy in copies[s + 2] if s + 2 < len(copies) else []:
        copy.start()


def forward_kernel(rows, cols, count, tiles, sketch, keep, send, held, sems):
    copies = fetch(tiles, held, sems)
    core = lax.axis_index("core")
    y = lax.axis_index("y")
    slots, tb, _ = held.shape
    depth = tb // PARTS
    keep[...] = jnp.zeros_like(keep)
    send[...] = jnp.zeros_like(send)
    for s in range(slots):
        await_tile(copies, s)

        def add(out):
            prod = dot(held[s], sketch[cols[s]], ((1,), (0,)))
            for p in range(PARTS):
                away = lax.rem(p - y + PARTS, PARTS)
                for h in range(2):
                    out[away, h] += prod[p * depth : (p + 1) * depth, h * SIDE : (h + 1) * SIDE]

        @pl.when((s < count[0]) & (rows[s] == core))
        def _():
            add(keep)

        @pl.when((s < count[0]) & (rows[s] != core))
        def _():
            add(send)


SMEM = pl.BlockSpec(memory_space=pltpu.SMEM)
VMEM = pl.BlockSpec(memory_space=pltpu.VMEM)
ANY = pl.BlockSpec(memory_space=pl.ANY)


def forward(rows, cols, count, tiles, sketch):
    slots, tb, _ = tiles.shape
    width = sketch.shape[-1]
    half = jax.ShapeDtypeStruct((PARTS, width // SIDE, tb // PARTS, SIDE), F32)
    return pl.pallas_call(
        forward_kernel,
        in_specs=[SMEM, SMEM, SMEM, ANY, VMEM],
        out_specs=[VMEM, VMEM],
        out_shape=[half, half],
        scratch_shapes=[pltpu.VMEM(tiles.shape, BF16), pltpu.SemaphoreType.DMA((slots, PARTS))],
        compiler_params=pltpu.CompilerParams(vmem_limit_bytes=LIMIT),
        name="forward",
    )(rows, cols, count, tiles, sketch)


def backward_kernel(rows, cols, count, tiles, *rest):
    own, other = rest[:PARTS], rest[PARTS : 2 * PARTS]
    outs = rest[2 * PARTS : 2 * PARTS + 4]
    out, flat, held, sems = rest[2 * PARTS + 4 :]
    copies = fetch(tiles, held, sems)
    core = lax.axis_index("core")
    y = lax.axis_index("y")
    here = 2 * lax.axis_index("row") + lax.axis_index("sk")
    slots, tb, _ = held.shape
    depth = tb // PARTS
    out[...] = jnp.zeros_like(out)
    for block, pieces in ((core, own), (1 - core, other)):
        for away, piece in enumerate(pieces):
            part = lax.rem(y - away + PARTS, PARTS)
            here_part = pl.ds(pl.multiple_of(part * depth, depth), depth)
            for h in range(piece.shape[0]):
                flat[block, h * SIDE : (h + 1) * SIDE, here_part] = piece[h].astype(BF16).T
    for s in range(slots):
        await_tile(copies, s)

        @pl.when(s < count[0])
        def _():
            prod = dot(flat[rows[s]], held[s], ((1,), (0,)))
            for q in range(2):
                for n in range(tb // 2 // SIDE):
                    at = q * (tb // 2) + n * SIDE
                    out[2 * cols[s] + q, n] += prod[:, at : at + SIDE]

    for n in range(4):
        outs[n][...] = out[here ^ n]


def backward(rows, cols, count, tiles, own, other):
    slots, tb, _ = tiles.shape
    width = own[0].shape[0] * SIDE
    quarter = (tb // 2 // SIDE, width, SIDE)
    return pl.pallas_call(
        backward_kernel,
        in_specs=[SMEM, SMEM, SMEM, ANY] + [VMEM] * (2 * PARTS),
        out_specs=[VMEM] * 4,
        out_shape=[jax.ShapeDtypeStruct(quarter, F32)] * 4,
        scratch_shapes=[
            pltpu.VMEM((4,) + quarter, F32),
            pltpu.VMEM((2, width, tb), BF16),
            pltpu.VMEM(tiles.shape, BF16),
            pltpu.SemaphoreType.DMA((slots, PARTS)),
        ],
        compiler_params=pltpu.CompilerParams(vmem_limit_bytes=LIMIT),
        name="backward",
    )(rows, cols, count, tiles, *own, *other)


def block_pairs(n):
    return [(i, j) for i in range(n) for j in range(i, n)]


def gram_kernel(*refs):
    zt, keep, send = refs[-3:]
    core = lax.axis_index("core")
    sk = lax.axis_index("sk")
    parts = refs[0:4]
    chunks, narrow, _ = refs[0].shape
    for far in range(2):
        rows = pl.ds(pl.multiple_of((sk ^ far) * narrow, narrow), narrow)
        for n in range(chunks):
            zt[rows, n * SIDE : (n + 1) * SIDE] = parts[far][n] + parts[far + 2][n]
    width = zt.shape[0]
    pairs = block_pairs(width // SIDE)
    half = len(pairs) // 2
    for i in range(width // SIDE):
        lhs = zt[i * SIDE : (i + 1) * SIDE, :]
        prod = dot(lhs, zt[i * SIDE :, :], ((1,), (1,)), HIGH)
        for n, (a, b) in enumerate(pairs):
            if a != i:
                continue
            block = prod[:, (b - i) * SIDE : (b - i + 1) * SIDE]

            @pl.when(core == n // half)
            def _():
                keep[n % half] = block

            @pl.when(core != n // half)
            def _():
                send[n % half] = block


def gram_of(parts):
    chunks, deep, _ = parts[0].shape
    width = 2 * deep
    half = len(block_pairs(width // SIDE)) // 2
    blocks = jax.ShapeDtypeStruct((half, SIDE, SIDE), F32)
    return pl.pallas_call(
        gram_kernel,
        in_specs=[VMEM] * len(parts),
        out_specs=[VMEM] * 3,
        out_shape=[jax.ShapeDtypeStruct((width, chunks * SIDE), F32), blocks, blocks],
        compiler_params=pltpu.CompilerParams(vmem_limit_bytes=LIMIT),
        name="gram",
    )(*parts)


def spread_rows(x, n):
    return jnp.broadcast_to(x[n : n + 1, :], (GROUP, SIDE))


def spread_lanes(x, n):
    return jnp.broadcast_to(x[:, n : n + 1], (GROUP, SIDE))


def eliminate(d, base):
    count = SUB // GROUP
    lanes = d.shape[1] // SIDE
    sub = lax.broadcasted_iota(jnp.int32, (GROUP, SIDE), 0)
    rows = [
        [d[base + GROUP * p : base + GROUP * (p + 1), SIDE * t : SIDE * (t + 1)] for t in range(lanes)]
        for p in range(count)
    ]

    def columns(b):
        first = base + GROUP * b
        return [[spread_lanes(rows[p][0], first + m) for p in range(b, count)] for m in range(GROUP)]

    cols = columns(0)
    for b in range(count):
        ahead = columns(b + 1) if b + 1 < count else []
        scale = jnp.zeros((GROUP, SIDE), F32)
        for m in range(GROUP):
            col = cols[m]
            inv = lax.rsqrt(spread_rows(col[0], m))
            inv2 = inv * inv
            for n in range(m + 1, GROUP):
                mult = spread_rows(col[0], n)
                cols[n] = [c - (l * mult) * inv2 for c, l in zip(cols[n], col)]
            scale = jnp.where(sub == m, inv, scale)
            low = [jnp.where(sub > m, col[0], 0.0) * inv2] + [l * inv2 for l in col[1:]]
            for n in range(len(ahead)):
                mult = spread_rows(col[1], n)
                ahead[n] = [c - l * mult for c, l in zip(ahead[n], low[1:])]
            for t in range(lanes):
                u = spread_rows(rows[b][t], m)
                for p in range(b, count):
                    rows[p][t] = rows[p][t] - low[p - b] * u
        for t in range(lanes):
            rows[b][t] = rows[b][t] * scale
        cols = ahead
    for p in range(count):
        for t in range(lanes):
            d[base + GROUP * p : base + GROUP * (p + 1), SIDE * t : SIDE * (t + 1)] = rows[p][t]


def cholesky_kernel(scale, own, other, upper, inverse, d):
    core = lax.axis_index("core")
    width = upper.shape[0]
    nb = width // SIDE
    pairs = block_pairs(nb)
    half = len(pairs) // 2
    upper[...] = jnp.zeros_like(upper)
    inverse[...] = jnp.zeros_like(inverse)
    for n, (i, j) in enumerate(pairs):
        spot = (slice(i * SIDE, (i + 1) * SIDE), slice(j * SIDE, (j + 1) * SIDE))

        @pl.when(core == n // half)
        def _():
            upper[spot] = own[n % half] * scale

        @pl.when(core != n // half)
        def _():
            upper[spot] = other[n % half] * scale

    row = lax.broadcasted_iota(jnp.int32, (SIDE, SIDE), 0)
    col = lax.broadcasted_iota(jnp.int32, (SIDE, SIDE), 1)
    eye = (row == col).astype(F32)

    def step(k, carry):
        here = pl.ds(pl.multiple_of(k * SIDE, SIDE), SIDE)
        d[:, 0:SIDE] = upper[here, here]
        d[:, SIDE:] = eye
        for s in range(SIDE // SUB):
            base = s * SUB
            eliminate(d, base)
            if base + SUB < SIDE:
                panel = d[base : base + SUB, :]
                left = panel[:, base + SUB : SIDE]
                d[base + SUB :, :] -= dot(left, panel, ((0,), (0,)), HIGH)
        upper[here, here] = jnp.where(row <= col, d[:, 0:SIDE], 0.0)
        inverse[here, here] = jnp.where(row >= col, d[:, SIDE:], 0.0)

        for kk in range(nb):

            @pl.when(k == kk)
            def _():
                lo, hi = kk * SIDE, (kk + 1) * SIDE
                w = inverse[lo:hi, lo:hi]
                if hi < width:
                    upper[lo:hi, hi:] = dot(w, upper[lo:hi, hi:], ((1,), (0,)), HIGH)
                if lo > 0:
                    inverse[lo:hi, 0:lo] = dot(w, inverse[lo:hi, 0:lo], ((1,), (0,)), HIGH)
                if hi < width:
                    left = upper[lo:hi, hi:].T
                    prod = dot(left, upper[lo:hi, hi:], ((1,), (0,)), HIGH)
                    for i in range(kk + 1, nb):
                        r = slice(i * SIDE, (i + 1) * SIDE)
                        o = slice((i - kk - 1) * SIDE, (i - kk) * SIDE)
                        upper[r, i * SIDE :] -= prod[o, (i - kk - 1) * SIDE :]
                    inverse[hi:, 0:hi] -= dot(left, inverse[lo:hi, 0:hi], ((1,), (0,)), HIGH)

        return carry

    lax.fori_loop(0, nb, step, 0)


def cholesky(own, other, total_rows, width):
    square = jax.ShapeDtypeStruct((width, width), F32)
    return pl.pallas_call(
        functools.partial(cholesky_kernel, 1.0 / total_rows),
        out_shape=[square, square],
        scratch_shapes=[pltpu.VMEM((SIDE, 2 * SIDE), F32)],
        compiler_params=pltpu.CompilerParams(vmem_limit_bytes=LIMIT),
        name="cholesky",
    )(own, other)


def split(x):
    high = x.astype(BF16)
    return high, (x - high.astype(F32)).astype(BF16)


def basis_kernel(inverse, quarters, out, held, done, load, store):
    chunk, narrow = done.shape[1:]
    loads = [pltpu.make_async_copy(quarters.at[n], held.at[n], load.at[n]) for n in range(4)]
    for copy in loads:
        copy.start()
    w = inverse[pl.ds(pl.multiple_of(lax.axis_index("sk") * narrow, narrow), narrow), :]
    w_high, w_low = split(w)
    stores = []
    for n in range(4):
        loads[n].wait()
        high, low = split(held[n])
        form = ((1,), (0,))
        done[n] = (dot(w_high, high, form) + (dot(w_high, low, form) + dot(w_low, high, form))).T
        stores.append(pltpu.make_async_copy(done.at[n], out.at[pl.ds(n * chunk, chunk), :], store.at[n]))
        stores[n].start()
    for copy in stores:
        copy.wait()


def basis_of(inverse, quarters):
    width = inverse.shape[0]
    narrow = width // 2
    chunk = quarters.shape[2]
    return pl.pallas_call(
        basis_kernel,
        in_specs=[VMEM, ANY],
        out_specs=ANY,
        out_shape=jax.ShapeDtypeStruct((4 * chunk, narrow), F32),
        scratch_shapes=[
            pltpu.VMEM((4, width, chunk), F32),
            pltpu.VMEM((4, chunk, narrow), F32),
            pltpu.SemaphoreType.DMA((4,)),
            pltpu.SemaphoreType.DMA((4,)),
        ],
        compiler_params=pltpu.CompilerParams(vmem_limit_bytes=LIMIT),
        name="basis",
    )(inverse, quarters)


def swap(x):
    return lax.ppermute(x, "core", [(0, 1), (1, 0)])


def shift(x, axes, n):
    size = lax.axis_size(axes)
    return lax.ppermute(x, axes, [(i, (i + n) % size) for i in range(size)])


def across(x, n):
    return lax.ppermute(x, RING, [(i, i ^ n) for i in range(4)])


def exchange(x, axes):
    return lax.all_to_all(x, axes, 0, 0, tiled=True)


def spread(x, axes):
    n = lax.axis_size(axes)
    return exchange(jnp.broadcast_to(x[None], (n,) + x.shape), axes)


def on_device(tiles, tile_rows, tile_cols, tile_count, sketch):
    blocks = tiles[0, 0]
    rows = tile_rows[0, 0]
    cols = tile_cols[0, 0]
    count = tile_count[0]
    tb = blocks.shape[1]
    narrow = sketch.shape[1]
    width = narrow * lax.axis_size("sk")
    total_rows = sketch.shape[0] * lax.axis_size(("z", "y", "core"))

    keep, send = forward(rows, cols, count, blocks, sketch.reshape(-1, tb, narrow))
    received = swap(send)
    pieces = [keep[n] + received[n] for n in range(PARTS)]
    for n in (1, 3, 2):
        pieces[n] = shift(pieces[n], "y", n)
    part = pieces[0] + pieces[1] + pieces[3] + pieces[2]
    deep = lax.axis_size("z")
    pieces = exchange(part.reshape(deep, -1, SIDE), "z")
    piece = jnp.sum(pieces, axis=0) * 0.75
    part = spread(piece, "z").reshape(part.shape)
    own = [part] + [shift(part, "y", n) for n in range(1, PARTS)]
    other = [swap(p) for p in own]
    pieces = backward(rows, cols, count, blocks, own, other)
    moved = [pieces[0]] + [across(pieces[n], n) for n in range(1, 4)]
    zt, keep, send = gram_of(moved)
    quarters = lax.all_gather(zt, RING, axis=0)

    half = keep + swap(send)
    sheet = lax.axis_size(SHEET)
    pieces = exchange(half.reshape(sheet, -1, SIDE), SHEET)
    piece = jnp.sum(pieces, axis=0)
    piece = jnp.sum(spread(piece, "z"), axis=0)
    own_g = spread(piece, SHEET).reshape(keep.shape)
    other_g = swap(own_g)

    upper, inverse = cholesky(own_g, other_g, total_rows, width)
    return basis_of(inverse, quarters), upper


def solution(mesh):
    fine = Mesh(mesh.devices.reshape(2, 8, 4, 2, 2), ("row", "z", "y", "core", "sk"))
    col = ("z", "y", "core")
    return jax.shard_map(
        on_device,
        mesh=fine,
        in_specs=(
            P("row", col, None, None, None),
            P("row", col, None),
            P("row", col, None),
            P("row", col),
            P(col, "sk"),
        ),
        out_specs=(P(col, "sk"), P()),
        check_vma=False,
    )
```

```python
import functools

import jax
import jax.numpy as jnp
from jax import lax
from jax.experimental import pallas as pl
from jax.experimental.pallas import tpu as pltpu
from jax.sharding import Mesh, PartitionSpec as P

HIGH = lax.Precision.HIGHEST
F32 = jnp.float32
BF16 = jnp.bfloat16
RING = ("row", "sk")
ODD = (1, 3)
SHEET = ("row", "y", "sk")
MIB = 1024 * 1024
SIDE = 128
GROUP = 8
SUB = 32


def dot(a, b, dims, precision=None):
    return lax.dot_general(a, b, (dims, ((), ())), precision=precision, preferred_element_type=F32)


PARTS = 4


def fetch(tiles, held, sems):
    slots, tb, _ = tiles.shape
    depth = tb // PARTS
    copies = [
        [
            pltpu.make_async_copy(
                tiles.at[s, pl.ds(p * depth, depth)], held.at[s, pl.ds(p * depth, depth)], sems.at[s, p]
            )
            for p in range(PARTS)
        ]
        for s in range(slots)
    ]
    for slot in copies:
        for copy in slot:
            copy.start()
    return copies


def forward_kernel(rows, cols, count, tiles, sketch, keep, send, held, sems):
    copies = fetch(tiles, held, sems)
    core = lax.axis_index("core")
    y = lax.axis_index("y")
    slots, tb, _ = held.shape
    depth = tb // PARTS
    keep[...] = jnp.zeros_like(keep)
    send[...] = jnp.zeros_like(send)
    for s in range(slots):
        for copy in copies[s]:
            copy.wait()

        def add(out):
            prod = dot(held[s], sketch[cols[s]], ((1,), (0,)))
            for p in range(PARTS):
                away = lax.rem(p - y + PARTS, PARTS)
                for h in range(2):
                    out[away, h] += prod[p * depth : (p + 1) * depth, h * SIDE : (h + 1) * SIDE]

        @pl.when((s < count[0]) & (rows[s] == core))
        def _():
            add(keep)

        @pl.when((s < count[0]) & (rows[s] != core))
        def _():
            add(send)


SMEM = pl.BlockSpec(memory_space=pltpu.SMEM)
VMEM = pl.BlockSpec(memory_space=pltpu.VMEM)
ANY = pl.BlockSpec(memory_space=pl.ANY)


def forward(rows, cols, count, tiles, sketch):
    slots, tb, _ = tiles.shape
    width = sketch.shape[-1]
    half = jax.ShapeDtypeStruct((PARTS, width // SIDE, tb // PARTS, SIDE), F32)
    return pl.pallas_call(
        forward_kernel,
        in_specs=[SMEM, SMEM, SMEM, ANY, VMEM],
        out_specs=[VMEM, VMEM],
        out_shape=[half, half],
        scratch_shapes=[pltpu.VMEM(tiles.shape, BF16), pltpu.SemaphoreType.DMA((slots, PARTS))],
        compiler_params=pltpu.CompilerParams(vmem_limit_bytes=48 * MIB),
        name="forward",
    )(rows, cols, count, tiles, sketch)


def backward_kernel(rows, cols, count, tiles, *rest):
    own, other = rest[:PARTS], rest[PARTS : 2 * PARTS]
    outs = rest[2 * PARTS : 2 * PARTS + 4]
    out, flat, held, sems = rest[2 * PARTS + 4 :]
    copies = fetch(tiles, held, sems)
    core = lax.axis_index("core")
    y = lax.axis_index("y")
    here = 2 * lax.axis_index("row") + lax.axis_index("sk")
    slots, tb, _ = held.shape
    depth = tb // PARTS
    out[...] = jnp.zeros_like(out)
    for block, pieces in ((core, own), (1 - core, other)):
        for away, piece in enumerate(pieces):
            part = lax.rem(y - away + PARTS, PARTS)
            here_part = pl.ds(pl.multiple_of(part * depth, depth), depth)
            for h in range(piece.shape[0]):
                flat[block, h * SIDE : (h + 1) * SIDE, here_part] = piece[h].astype(BF16).T
    for s in range(slots):
        for copy in copies[s]:
            copy.wait()

        @pl.when(s < count[0])
        def _():
            prod = dot(flat[rows[s]], held[s], ((1,), (0,)))
            for q in range(2):
                for n in range(tb // 2 // SIDE):
                    at = q * (tb // 2) + n * SIDE
                    out[2 * cols[s] + q, n] += prod[:, at : at + SIDE]

    for n in range(4):
        outs[n][...] = out[here ^ n]


def backward(rows, cols, count, tiles, own, other):
    slots, tb, _ = tiles.shape
    width = own[0].shape[0] * SIDE
    quarter = (tb // 2 // SIDE, width, SIDE)
    return pl.pallas_call(
        backward_kernel,
        in_specs=[SMEM, SMEM, SMEM, ANY] + [VMEM] * (2 * PARTS),
        out_specs=[VMEM] * 4,
        out_shape=[jax.ShapeDtypeStruct(quarter, F32)] * 4,
        scratch_shapes=[
            pltpu.VMEM((4,) + quarter, F32),
            pltpu.VMEM((2, width, tb), BF16),
            pltpu.VMEM(tiles.shape, BF16),
            pltpu.SemaphoreType.DMA((slots, PARTS)),
        ],
        compiler_params=pltpu.CompilerParams(vmem_limit_bytes=48 * MIB),
        name="backward",
    )(rows, cols, count, tiles, *own, *other)


def block_pairs(n):
    return [(i, j) for i in range(n) for j in range(i, n)]


def gram_kernel(*refs):
    low, high, keep, send, zt = refs[-5:]
    core = lax.axis_index("core")
    sk = lax.axis_index("sk")
    parts = refs[0:4]
    chunks, narrow, _ = refs[0].shape
    for far in range(2):
        rows = pl.ds(pl.multiple_of((sk ^ far) * narrow, narrow), narrow)
        for n in range(chunks):
            zt[rows, n * SIDE : (n + 1) * SIDE] = parts[far][n] + parts[far + 2][n]
    low[...] = zt[0:narrow, :]
    high[...] = zt[narrow:, :]
    width = zt.shape[0]
    pairs = block_pairs(width // SIDE)
    half = len(pairs) // 2
    for i in range(width // SIDE):
        lhs = zt[i * SIDE : (i + 1) * SIDE, :]
        prod = dot(lhs, zt[i * SIDE :, :], ((1,), (1,)), HIGH)
        for n, (a, b) in enumerate(pairs):
            if a != i:
                continue
            block = prod[:, (b - i) * SIDE : (b - i + 1) * SIDE]

            @pl.when(core == n // half)
            def _():
                keep[n % half] = block

            @pl.when(core != n // half)
            def _():
                send[n % half] = block


def gram_of(parts):
    chunks, deep, _ = parts[0].shape
    width = 2 * deep
    half = len(block_pairs(width // SIDE)) // 2
    blocks = jax.ShapeDtypeStruct((half, SIDE, SIDE), F32)
    return pl.pallas_call(
        gram_kernel,
        in_specs=[VMEM] * len(parts),
        out_specs=[VMEM] * 4,
        out_shape=[jax.ShapeDtypeStruct((deep, chunks * SIDE), F32)] * 2 + [blocks, blocks],
        scratch_shapes=[pltpu.VMEM((width, chunks * SIDE), F32)],
        compiler_params=pltpu.CompilerParams(vmem_limit_bytes=32 * MIB),
        name="gram",
    )(*parts)


def spread_rows(x, n):
    return jnp.broadcast_to(x[n : n + 1, :], (GROUP, SIDE))


def spread_lanes(x, n):
    return jnp.broadcast_to(x[:, n : n + 1], (GROUP, SIDE))


def eliminate(d, base):
    count = SUB // GROUP
    lanes = d.shape[1] // SIDE
    sub = lax.broadcasted_iota(jnp.int32, (GROUP, SIDE), 0)
    rows = [
        [d[base + GROUP * p : base + GROUP * (p + 1), SIDE * t : SIDE * (t + 1)] for t in range(lanes)]
        for p in range(count)
    ]

    def columns(b):
        first = base + GROUP * b
        return [[spread_lanes(rows[p][0], first + m) for p in range(b, count)] for m in range(GROUP)]

    cols = columns(0)
    for b in range(count):
        ahead = columns(b + 1) if b + 1 < count else []
        scale = jnp.zeros((GROUP, SIDE), F32)
        for m in range(GROUP):
            col = cols[m]
            inv = lax.rsqrt(spread_rows(col[0], m))
            inv2 = inv * inv
            for n in range(m + 1, GROUP):
                mult = spread_rows(col[0], n)
                cols[n] = [c - (l * mult) * inv2 for c, l in zip(cols[n], col)]
            scale = jnp.where(sub == m, inv, scale)
            low = [jnp.where(sub > m, col[0], 0.0) * inv2] + [l * inv2 for l in col[1:]]
            for n in range(len(ahead)):
                mult = spread_rows(col[1], n)
                ahead[n] = [c - l * mult for c, l in zip(ahead[n], low[1:])]
            for t in range(lanes):
                u = spread_rows(rows[b][t], m)
                for p in range(b, count):
                    rows[p][t] = rows[p][t] - low[p - b] * u
        for t in range(lanes):
            rows[b][t] = rows[b][t] * scale
        cols = ahead
    for p in range(count):
        for t in range(lanes):
            d[base + GROUP * p : base + GROUP * (p + 1), SIDE * t : SIDE * (t + 1)] = rows[p][t]


def cholesky_kernel(scale, own, other, upper, inverse, d):
    core = lax.axis_index("core")
    width = upper.shape[0]
    nb = width // SIDE
    pairs = block_pairs(nb)
    half = len(pairs) // 2
    upper[...] = jnp.zeros_like(upper)
    inverse[...] = jnp.zeros_like(inverse)
    for n, (i, j) in enumerate(pairs):
        spot = (slice(i * SIDE, (i + 1) * SIDE), slice(j * SIDE, (j + 1) * SIDE))

        @pl.when(core == n // half)
        def _():
            upper[spot] = own[n % half] * scale

        @pl.when(core != n // half)
        def _():
            upper[spot] = other[n % half] * scale

    row = lax.broadcasted_iota(jnp.int32, (SIDE, SIDE), 0)
    col = lax.broadcasted_iota(jnp.int32, (SIDE, SIDE), 1)
    eye = (row == col).astype(F32)

    def step(k, carry):
        here = pl.ds(pl.multiple_of(k * SIDE, SIDE), SIDE)
        d[:, 0:SIDE] = upper[here, here]
        d[:, SIDE:] = eye
        for s in range(SIDE // SUB):
            base = s * SUB
            eliminate(d, base)
            if base + SUB < SIDE:
                panel = d[base : base + SUB, :]
                left = panel[:, base + SUB : SIDE]
                d[base + SUB :, :] -= dot(left, panel, ((0,), (0,)), HIGH)
        upper[here, here] = jnp.where(row <= col, d[:, 0:SIDE], 0.0)
        inverse[here, here] = jnp.where(row >= col, d[:, SIDE:], 0.0)

        for kk in range(nb):

            @pl.when(k == kk)
            def _():
                lo, hi = kk * SIDE, (kk + 1) * SIDE
                w = inverse[lo:hi, lo:hi]
                if hi < width:
                    upper[lo:hi, hi:] = dot(w, upper[lo:hi, hi:], ((1,), (0,)), HIGH)
                if lo > 0:
                    inverse[lo:hi, 0:lo] = dot(w, inverse[lo:hi, 0:lo], ((1,), (0,)), HIGH)
                if hi < width:
                    left = upper[lo:hi, hi:].T
                    prod = dot(left, upper[lo:hi, hi:], ((1,), (0,)), HIGH)
                    for i in range(kk + 1, nb):
                        r = slice(i * SIDE, (i + 1) * SIDE)
                        o = slice((i - kk - 1) * SIDE, (i - kk) * SIDE)
                        upper[r, i * SIDE :] -= prod[o, (i - kk - 1) * SIDE :]
                    inverse[hi:, 0:hi] -= dot(left, inverse[lo:hi, 0:hi], ((1,), (0,)), HIGH)

        return carry

    lax.fori_loop(0, nb, step, 0)


def cholesky(own, other, total_rows, width):
    square = jax.ShapeDtypeStruct((width, width), F32)
    return pl.pallas_call(
        functools.partial(cholesky_kernel, 1.0 / total_rows),
        out_shape=[square, square],
        scratch_shapes=[pltpu.VMEM((SIDE, 2 * SIDE), F32)],
        compiler_params=pltpu.CompilerParams(vmem_limit_bytes=24 * MIB),
        cost_estimate=pl.CostEstimate(flops=2**34, bytes_accessed=2**22, transcendentals=0),
        name="cholesky",
    )(own, other)


def split(x):
    high = x.astype(BF16)
    return high, (x - high.astype(F32)).astype(BF16)


def basis_kernel(inverse, *refs):
    lows, highs = refs[0:4], refs[4:8]
    out, done, store = refs[8:]
    here = 2 * lax.axis_index("row") + lax.axis_index("sk")
    chunk, narrow = done.shape[1:]
    form = ((1,), (0,))
    rows = pl.ds(pl.multiple_of(lax.axis_index("sk") * narrow, narrow), narrow)
    weights = [split(inverse[rows, k * narrow : (k + 1) * narrow]) for k in range(2)]
    stores = []
    for n in range(4):
        total = 0.0
        for (w_high, w_low), part in zip(weights, (lows[n], highs[n])):
            high, low = split(part[...])
            total += dot(w_high, high, form) + (dot(w_high, low, form) + dot(w_low, high, form))
        done[n] = total.T
        place = pl.ds(pl.multiple_of((here ^ n) * chunk, chunk), chunk)
        stores.append(pltpu.make_async_copy(done.at[n], out.at[place, :], store.at[n]))
        stores[n].start()
    for copy in stores:
        copy.wait()


def basis_of(inverse, lows, highs):
    narrow, chunk = lows[0].shape
    return pl.pallas_call(
        basis_kernel,
        in_specs=[VMEM] * 9,
        out_specs=ANY,
        out_shape=jax.ShapeDtypeStruct((4 * chunk, narrow), F32),
        scratch_shapes=[pltpu.VMEM((4, chunk, narrow), F32), pltpu.SemaphoreType.DMA((4,))],
        compiler_params=pltpu.CompilerParams(vmem_limit_bytes=32 * MIB),
        name="basis",
    )(inverse, *lows, *highs)


def swap(x):
    return lax.ppermute(x, "core", [(0, 1), (1, 0)])


def shift(x, axes, n):
    size = lax.axis_size(axes)
    return lax.ppermute(x, axes, [(i, (i + n) % size) for i in range(size)])


def across(x, n, to=range(4)):
    return lax.ppermute(x, RING, [(i ^ n, i) for i in to])


def exchange(x, axes):
    return lax.all_to_all(x, axes, 0, 0, tiled=True)


def spread(x, axes):
    n = lax.axis_size(axes)
    return exchange(jnp.broadcast_to(x[None], (n,) + x.shape), axes)


def on_device(tiles, tile_rows, tile_cols, tile_count, sketch):
    blocks = tiles[0, 0]
    rows = tile_rows[0, 0]
    cols = tile_cols[0, 0]
    count = tile_count[0]
    tb = blocks.shape[1]
    narrow = sketch.shape[1]
    width = narrow * lax.axis_size("sk")
    total_rows = sketch.shape[0] * lax.axis_size(("z", "y", "core"))

    keep, send = forward(rows, cols, count, blocks, sketch.reshape(-1, tb, narrow))
    received = swap(send)
    pieces = [keep[n] + received[n] for n in range(PARTS)]
    for n in (1, 3, 2):
        pieces[n] = shift(pieces[n], "y", n)
    part = pieces[0] + pieces[1] + pieces[3] + pieces[2]
    deep = lax.axis_size("z")
    pieces = exchange(part.reshape(deep, -1, SIDE), "z")
    piece = jnp.sum(pieces, axis=0) * 0.75
    part = spread(piece, "z").reshape(part.shape)
    own = [part] + [shift(part, "y", n) for n in range(1, PARTS)]
    other = [swap(p) for p in own]
    pieces = backward(rows, cols, count, blocks, own, other)
    moved = [pieces[0]] + [across(pieces[n], n) for n in range(1, 4)]
    low, high, keep, send = gram_of(moved)

    lows = [low, across(low, 1), None, across(low, 3)]
    half = keep + swap(send)
    sheet = lax.axis_size(SHEET)
    pieces = exchange(half.reshape(sheet, -1, SIDE), SHEET)
    piece, lows[1], lows[3] = lax.optimization_barrier((jnp.sum(pieces, axis=0), lows[1], lows[3]))
    late, _ = lax.optimization_barrier((high, piece))
    highs = [high, across(late, 1, ODD), None, across(late, 3, ODD)]
    piece = jnp.sum(spread(piece, "z"), axis=0)
    piece, highs[1], highs[3] = lax.optimization_barrier((piece, highs[1], highs[3]))
    own_g = spread(piece, SHEET).reshape(keep.shape)
    late, latest, _ = lax.optimization_barrier((low, high, own_g))
    lows[2] = across(late, 2)
    highs[2] = across(latest, 2, ODD)
    other_g = swap(own_g)

    upper, inverse = cholesky(own_g, other_g, total_rows, width)
    return basis_of(inverse, lows, highs), upper


def solution(mesh):
    fine = Mesh(mesh.devices.reshape(2, 8, 4, 2, 2), ("row", "z", "y", "core", "sk"))
    col = ("z", "y", "core")
    return jax.shard_map(
        on_device,
        mesh=fine,
        in_specs=(
            P("row", col, None, None, None),
            P("row", col, None),
            P("row", col, None),
            P("row", col),
            P(col, "sk"),
        ),
        out_specs=(P(col, "sk"), P()),
        check_vma=False,
    )
```

```python
import functools

import jax
import jax.numpy as jnp
from jax import lax
from jax.experimental import pallas as pl
from jax.experimental.pallas import tpu as pltpu
from jax.sharding import Mesh, PartitionSpec as P

HIGH = lax.Precision.HIGHEST
F32 = jnp.float32
BF16 = jnp.bfloat16
RING = ("row", "sk")
ODD = (1, 3)
SHEET = ("row", "y", "sk")
MIB = 1024 * 1024
SIDE = 128
GROUP = 8
SUB = 32


def dot(a, b, dims, precision=None):
    return lax.dot_general(a, b, (dims, ((), ())), precision=precision, preferred_element_type=F32)


PARTS = 4


def fetch(tiles, held, sems):
    slots, tb, _ = tiles.shape
    depth = tb // PARTS
    copies = [
        [
            pltpu.make_async_copy(
                tiles.at[s, pl.ds(p * depth, depth)], held.at[s, pl.ds(p * depth, depth)], sems.at[s, p]
            )
            for p in range(PARTS)
        ]
        for s in range(slots)
    ]
    for slot in copies:
        for copy in slot:
            copy.start()
    return copies


def forward_kernel(rows, cols, count, tiles, sketch, keep, send, held, sems):
    copies = fetch(tiles, held, sems)
    core = lax.axis_index("core")
    y = lax.axis_index("y")
    slots, tb, _ = held.shape
    depth = tb // PARTS
    keep[...] = jnp.zeros_like(keep)
    send[...] = jnp.zeros_like(send)
    for s in range(slots):
        for copy in copies[s]:
            copy.wait()

        def add(out):
            prod = dot(held[s], sketch[cols[s]], ((1,), (0,)))
            for p in range(PARTS):
                away = lax.rem(p - y + PARTS, PARTS)
                for h in range(2):
                    out[away, h] += prod[p * depth : (p + 1) * depth, h * SIDE : (h + 1) * SIDE]

        @pl.when((s < count[0]) & (rows[s] == core))
        def _():
            add(keep)

        @pl.when((s < count[0]) & (rows[s] != core))
        def _():
            add(send)


SMEM = pl.BlockSpec(memory_space=pltpu.SMEM)
VMEM = pl.BlockSpec(memory_space=pltpu.VMEM)
ANY = pl.BlockSpec(memory_space=pl.ANY)


def forward(rows, cols, count, tiles, sketch):
    slots, tb, _ = tiles.shape
    width = sketch.shape[-1]
    half = jax.ShapeDtypeStruct((PARTS, width // SIDE, tb // PARTS, SIDE), F32)
    return pl.pallas_call(
        forward_kernel,
        in_specs=[SMEM, SMEM, SMEM, ANY, VMEM],
        out_specs=[VMEM, VMEM],
        out_shape=[half, half],
        scratch_shapes=[pltpu.VMEM(tiles.shape, BF16), pltpu.SemaphoreType.DMA((slots, PARTS))],
        compiler_params=pltpu.CompilerParams(vmem_limit_bytes=48 * MIB),
        name="forward",
    )(rows, cols, count, tiles, sketch)


def backward_kernel(rows, cols, count, tiles, *rest):
    own, other = rest[:PARTS], rest[PARTS : 2 * PARTS]
    outs = rest[2 * PARTS : 2 * PARTS + 4]
    out, flat, held, sems = rest[2 * PARTS + 4 :]
    copies = fetch(tiles, held, sems)
    core = lax.axis_index("core")
    y = lax.axis_index("y")
    here = 2 * lax.axis_index("row") + lax.axis_index("sk")
    slots, tb, _ = held.shape
    depth = tb // PARTS
    out[...] = jnp.zeros_like(out)
    for block, pieces in ((core, own), (1 - core, other)):
        for away, piece in enumerate(pieces):
            part = lax.rem(y - away + PARTS, PARTS)
            here_part = pl.ds(pl.multiple_of(part * depth, depth), depth)
            for h in range(piece.shape[0]):
                flat[block, h * SIDE : (h + 1) * SIDE, here_part] = piece[h].astype(BF16).T
    for s in range(slots):
        for copy in copies[s]:
            copy.wait()

        @pl.when(s < count[0])
        def _():
            prod = dot(flat[rows[s]], held[s], ((1,), (0,)))
            for q in range(2):
                for n in range(tb // 2 // SIDE):
                    at = q * (tb // 2) + n * SIDE
                    out[2 * cols[s] + q, n] += prod[:, at : at + SIDE]

    for n in range(4):
        outs[n][...] = out[here ^ n]


def backward(rows, cols, count, tiles, own, other):
    slots, tb, _ = tiles.shape
    width = own[0].shape[0] * SIDE
    quarter = (tb // 2 // SIDE, width, SIDE)
    return pl.pallas_call(
        backward_kernel,
        in_specs=[SMEM, SMEM, SMEM, ANY] + [VMEM] * (2 * PARTS),
        out_specs=[VMEM] * 4,
        out_shape=[jax.ShapeDtypeStruct(quarter, F32)] * 4,
        scratch_shapes=[
            pltpu.VMEM((4,) + quarter, F32),
            pltpu.VMEM((2, width, tb), BF16),
            pltpu.VMEM(tiles.shape, BF16),
            pltpu.SemaphoreType.DMA((slots, PARTS)),
        ],
        compiler_params=pltpu.CompilerParams(vmem_limit_bytes=48 * MIB),
        name="backward",
    )(rows, cols, count, tiles, *own, *other)


def block_pairs(n):
    return [(i, j) for i in range(n) for j in range(i, n)]


def gram_kernel(*refs):
    low, high, keep, send, zt = refs[-5:]
    core = lax.axis_index("core")
    sk = lax.axis_index("sk")
    parts = refs[0:4]
    chunks, narrow, _ = refs[0].shape
    for far in range(2):
        rows = pl.ds(pl.multiple_of((sk ^ far) * narrow, narrow), narrow)
        for n in range(chunks):
            zt[rows, n * SIDE : (n + 1) * SIDE] = parts[far][n] + parts[far + 2][n]
    low[...] = zt[0:narrow, :]
    high[...] = zt[narrow:, :]
    width = zt.shape[0]
    pairs = block_pairs(width // SIDE)
    half = len(pairs) // 2
    for i in range(width // SIDE):
        lhs = zt[i * SIDE : (i + 1) * SIDE, :]
        prod = dot(lhs, zt[i * SIDE :, :], ((1,), (1,)), HIGH)
        for n, (a, b) in enumerate(pairs):
            if a != i:
                continue
            block = prod[:, (b - i) * SIDE : (b - i + 1) * SIDE]

            @pl.when(core == n // half)
            def _():
                keep[n % half] = block

            @pl.when(core != n // half)
            def _():
                send[n % half] = block


def gram_of(parts):
    chunks, deep, _ = parts[0].shape
    width = 2 * deep
    half = len(block_pairs(width // SIDE)) // 2
    blocks = jax.ShapeDtypeStruct((half, SIDE, SIDE), F32)
    return pl.pallas_call(
        gram_kernel,
        in_specs=[VMEM] * len(parts),
        out_specs=[VMEM] * 4,
        out_shape=[jax.ShapeDtypeStruct((deep, chunks * SIDE), F32)] * 2 + [blocks, blocks],
        scratch_shapes=[pltpu.VMEM((width, chunks * SIDE), F32)],
        compiler_params=pltpu.CompilerParams(vmem_limit_bytes=32 * MIB),
        name="gram",
    )(*parts)


def spread_rows(x, n):
    return jnp.broadcast_to(x[n : n + 1, :], (GROUP, SIDE))


def spread_lanes(x, n):
    return jnp.broadcast_to(x[:, n : n + 1], (GROUP, SIDE))


def eliminate(d, base):
    count = SUB // GROUP
    lanes = d.shape[1] // SIDE
    sub = lax.broadcasted_iota(jnp.int32, (GROUP, SIDE), 0)
    rows = [
        [d[base + GROUP * p : base + GROUP * (p + 1), SIDE * t : SIDE * (t + 1)] for t in range(lanes)]
        for p in range(count)
    ]

    def columns(b):
        first = base + GROUP * b
        return [[spread_lanes(rows[p][0], first + m) for p in range(b, count)] for m in range(GROUP)]

    cols = columns(0)
    for b in range(count):
        ahead = columns(b + 1) if b + 1 < count else []
        scale = jnp.zeros((GROUP, SIDE), F32)
        for m in range(GROUP):
            col = cols[m]
            inv = lax.rsqrt(spread_rows(col[0], m))
            inv2 = inv * inv
            for n in range(m + 1, GROUP):
                mult = spread_rows(col[0], n)
                cols[n] = [c - (l * mult) * inv2 for c, l in zip(cols[n], col)]
            scale = jnp.where(sub == m, inv, scale)
            low = [jnp.where(sub > m, col[0], 0.0) * inv2] + [l * inv2 for l in col[1:]]
            for n in range(len(ahead)):
                mult = spread_rows(col[1], n)
                ahead[n] = [c - l * mult for c, l in zip(ahead[n], low[1:])]
            for t in range(lanes):
                u = spread_rows(rows[b][t], m)
                for p in range(b, count):
                    rows[p][t] = rows[p][t] - low[p - b] * u
        for t in range(lanes):
            rows[b][t] = rows[b][t] * scale
        cols = ahead
    for p in range(count):
        for t in range(lanes):
            d[base + GROUP * p : base + GROUP * (p + 1), SIDE * t : SIDE * (t + 1)] = rows[p][t]


def cholesky_kernel(scale, own, other, upper, inverse, d):
    core = lax.axis_index("core")
    width = upper.shape[0]
    nb = width // SIDE
    pairs = block_pairs(nb)
    half = len(pairs) // 2
    upper[...] = jnp.zeros_like(upper)
    inverse[...] = jnp.zeros_like(inverse)
    for n, (i, j) in enumerate(pairs):
        spot = (slice(i * SIDE, (i + 1) * SIDE), slice(j * SIDE, (j + 1) * SIDE))

        @pl.when(core == n // half)
        def _():
            upper[spot] = own[n % half] * scale

        @pl.when(core != n // half)
        def _():
            upper[spot] = other[n % half] * scale

    row = lax.broadcasted_iota(jnp.int32, (SIDE, SIDE), 0)
    col = lax.broadcasted_iota(jnp.int32, (SIDE, SIDE), 1)
    eye = (row == col).astype(F32)

    def step(k, carry):
        here = pl.ds(pl.multiple_of(k * SIDE, SIDE), SIDE)
        d[:, 0:SIDE] = upper[here, here]
        d[:, SIDE:] = eye
        for s in range(SIDE // SUB):
            base = s * SUB
            eliminate(d, base)
            if base + SUB < SIDE:
                panel = d[base : base + SUB, :]
                left = panel[:, base + SUB : SIDE]
                d[base + SUB :, :] -= dot(left, panel, ((0,), (0,)), HIGH)
        upper[here, here] = jnp.where(row <= col, d[:, 0:SIDE], 0.0)
        inverse[here, here] = jnp.where(row >= col, d[:, SIDE:], 0.0)

        for kk in range(nb):

            @pl.when(k == kk)
            def _():
                lo, hi = kk * SIDE, (kk + 1) * SIDE
                w = inverse[lo:hi, lo:hi]
                if hi < width:
                    upper[lo:hi, hi:] = dot(w, upper[lo:hi, hi:], ((1,), (0,)), HIGH)
                if lo > 0:
                    inverse[lo:hi, 0:lo] = dot(w, inverse[lo:hi, 0:lo], ((1,), (0,)), HIGH)
                if hi < width:
                    left = upper[lo:hi, hi:].T
                    prod = dot(left, upper[lo:hi, hi:], ((1,), (0,)), HIGH)
                    for i in range(kk + 1, nb):
                        r = slice(i * SIDE, (i + 1) * SIDE)
                        o = slice((i - kk - 1) * SIDE, (i - kk) * SIDE)
                        upper[r, i * SIDE :] -= prod[o, (i - kk - 1) * SIDE :]
                    inverse[hi:, 0:hi] -= dot(left, inverse[lo:hi, 0:hi], ((1,), (0,)), HIGH)

        return carry

    lax.fori_loop(0, nb, step, 0)


def cholesky(own, other, total_rows, width):
    square = jax.ShapeDtypeStruct((width, width), F32)
    return pl.pallas_call(
        functools.partial(cholesky_kernel, 1.0 / total_rows),
        out_shape=[square, square],
        scratch_shapes=[pltpu.VMEM((SIDE, 2 * SIDE), F32)],
        compiler_params=pltpu.CompilerParams(vmem_limit_bytes=24 * MIB),
        cost_estimate=pl.CostEstimate(flops=2**34, bytes_accessed=2**22, transcendentals=0),
        name="cholesky",
    )(own, other)


def split(x):
    high = x.astype(BF16)
    return high, (x - high.astype(F32)).astype(BF16)


def basis_kernel(inverse, *refs):
    lows = [refs[0:1], refs[1:2], refs[2:4], refs[4:5]]
    highs = refs[5:9]
    out, done, store = refs[9:]
    here = 2 * lax.axis_index("row") + lax.axis_index("sk")
    chunk, narrow = done.shape[1:]
    form = ((1,), (0,))
    rows = pl.ds(pl.multiple_of(lax.axis_index("sk") * narrow, narrow), narrow)
    weights = [split(inverse[rows, k * narrow : (k + 1) * narrow]) for k in range(2)]
    stores = []
    for n in range(4):
        total = 0.0
        parts = (jnp.concatenate([ref[...] for ref in lows[n]], axis=0), highs[n][...])
        for (w_high, w_low), part in zip(weights, parts):
            high, low = split(part)
            total += dot(w_high, high, form) + (dot(w_high, low, form) + dot(w_low, high, form))
        done[n] = total.T
        place = pl.ds(pl.multiple_of((here ^ n) * chunk, chunk), chunk)
        stores.append(pltpu.make_async_copy(done.at[n], out.at[place, :], store.at[n]))
        stores[n].start()
    for copy in stores:
        copy.wait()


def basis_of(inverse, lows, highs):
    narrow, chunk = lows[0].shape
    return pl.pallas_call(
        basis_kernel,
        in_specs=[VMEM] * 10,
        out_specs=ANY,
        out_shape=jax.ShapeDtypeStruct((4 * chunk, narrow), F32),
        scratch_shapes=[pltpu.VMEM((4, chunk, narrow), F32), pltpu.SemaphoreType.DMA((4,))],
        compiler_params=pltpu.CompilerParams(vmem_limit_bytes=32 * MIB),
        name="basis",
    )(inverse, *lows, *highs)


def swap(x):
    return lax.ppermute(x, "core", [(0, 1), (1, 0)])


def shift(x, axes, n):
    size = lax.axis_size(axes)
    return lax.ppermute(x, axes, [(i, (i + n) % size) for i in range(size)])


def across(x, n, to=range(4)):
    return lax.ppermute(x, RING, [(i ^ n, i) for i in to])


def exchange(x, axes):
    return lax.all_to_all(x, axes, 0, 0, tiled=True)


def spread(x, axes):
    n = lax.axis_size(axes)
    return exchange(jnp.broadcast_to(x[None], (n,) + x.shape), axes)


def on_device(tiles, tile_rows, tile_cols, tile_count, sketch):
    blocks = tiles[0, 0]
    rows = tile_rows[0, 0]
    cols = tile_cols[0, 0]
    count = tile_count[0]
    tb = blocks.shape[1]
    narrow = sketch.shape[1]
    width = narrow * lax.axis_size("sk")
    total_rows = sketch.shape[0] * lax.axis_size(("z", "y", "core"))

    keep, send = forward(rows, cols, count, blocks, sketch.reshape(-1, tb, narrow))
    received = swap(send)
    pieces = [keep[n] + received[n] for n in range(PARTS)]
    for n in (1, 3, 2):
        pieces[n] = shift(pieces[n], "y", n)
    part = pieces[0] + pieces[1] + pieces[3] + pieces[2]
    deep = lax.axis_size("z")
    pieces = exchange(part.reshape(deep, -1, SIDE), "z")
    piece = jnp.sum(pieces, axis=0) * 0.75
    part = spread(piece, "z").reshape(part.shape)
    own = [part] + [shift(part, "y", n) for n in range(1, PARTS)]
    other = [swap(p) for p in own]
    pieces = backward(rows, cols, count, blocks, own, other)
    moved = [pieces[0]] + [across(pieces[n], n) for n in range(1, 4)]
    low, high, keep, send = gram_of(moved)

    lows = [low, across(low, 1), None, across(low, 3)]
    half = keep + swap(send)
    sheet = lax.axis_size(SHEET)
    pieces = exchange(half.reshape(sheet, -1, SIDE), SHEET)
    piece, lows[1], lows[3] = lax.optimization_barrier((jnp.sum(pieces, axis=0), lows[1], lows[3]))
    late, _ = lax.optimization_barrier((high, piece))
    highs = [high, across(late, 1, ODD), None, across(late, 3, ODD)]
    piece = jnp.sum(spread(piece, "z"), axis=0)
    piece, highs[1], highs[3] = lax.optimization_barrier((piece, highs[1], highs[3]))
    own_g = spread(piece, SHEET).reshape(keep.shape)
    first, second, late, _ = lax.optimization_barrier((lows[3], lows[1], high, own_g))
    middle = narrow // 2
    relayed = [across(first[:middle], 1), across(second[middle:], 3)]
    lows[2] = None
    highs[2] = across(late, 2, ODD)
    other_g = swap(own_g)

    upper, inverse = cholesky(own_g, other_g, total_rows, width)
    return basis_of(inverse, lows[:2] + relayed + lows[3:], highs), upper


def solution(mesh):
    fine = Mesh(mesh.devices.reshape(2, 8, 4, 2, 2), ("row", "z", "y", "core", "sk"))
    col = ("z", "y", "core")
    return jax.shard_map(
        on_device,
        mesh=fine,
        in_specs=(
            P("row", col, None, None, None),
            P("row", col, None),
            P("row", col, None),
            P("row", col),
            P(col, "sk"),
        ),
        out_specs=(P(col, "sk"), P()),
        check_vma=False,
    )
```

```python
import functools

import jax
import jax.numpy as jnp
from jax import lax
from jax.experimental import pallas as pl
from jax.experimental.pallas import tpu as pltpu
from jax.sharding import Mesh, PartitionSpec as P

HIGH = lax.Precision.HIGHEST
F32 = jnp.float32
BF16 = jnp.bfloat16
RING = ("row", "sk")
ODD = (1, 3)
SHEET = ("row", "y", "sk")
MIB = 1024 * 1024
SIDE = 128
GROUP = 8
SUB = 32


def dot(a, b, dims, precision=None):
    return lax.dot_general(a, b, (dims, ((), ())), precision=precision, preferred_element_type=F32)


PARTS = 4


def fetch(tiles, held, sems):
    slots, tb, _ = tiles.shape
    depth = tb // PARTS
    copies = [
        [
            pltpu.make_async_copy(
                tiles.at[s, pl.ds(p * depth, depth)], held.at[s, pl.ds(p * depth, depth)], sems.at[s, p]
            )
            for p in range(PARTS)
        ]
        for s in range(slots)
    ]
    for slot in copies:
        for copy in slot:
            copy.start()
    return copies


def forward_kernel(rows, cols, count, tiles, sketch, keep, send, held, sems):
    copies = fetch(tiles, held, sems)
    core = lax.axis_index("core")
    y = lax.axis_index("y")
    slots, tb, _ = held.shape
    depth = tb // PARTS
    keep[...] = jnp.zeros_like(keep)
    send[...] = jnp.zeros_like(send)
    for s in range(slots):
        for copy in copies[s]:
            copy.wait()

        def add(out):
            prod = dot(held[s], sketch[cols[s]], ((1,), (0,)))
            for p in range(PARTS):
                away = lax.rem(p - y + PARTS, PARTS)
                for h in range(2):
                    out[away, h] += prod[p * depth : (p + 1) * depth, h * SIDE : (h + 1) * SIDE]

        @pl.when((s < count[0]) & (rows[s] == core))
        def _():
            add(keep)

        @pl.when((s < count[0]) & (rows[s] != core))
        def _():
            add(send)


SMEM = pl.BlockSpec(memory_space=pltpu.SMEM)
VMEM = pl.BlockSpec(memory_space=pltpu.VMEM)
ANY = pl.BlockSpec(memory_space=pl.ANY)


def forward(rows, cols, count, tiles, sketch):
    slots, tb, _ = tiles.shape
    width = sketch.shape[-1]
    half = jax.ShapeDtypeStruct((PARTS, width // SIDE, tb // PARTS, SIDE), F32)
    return pl.pallas_call(
        forward_kernel,
        in_specs=[SMEM, SMEM, SMEM, ANY, VMEM],
        out_specs=[VMEM, VMEM],
        out_shape=[half, half],
        scratch_shapes=[pltpu.VMEM(tiles.shape, BF16), pltpu.SemaphoreType.DMA((slots, PARTS))],
        compiler_params=pltpu.CompilerParams(vmem_limit_bytes=48 * MIB),
        name="forward",
    )(rows, cols, count, tiles, sketch)


def backward_kernel(rows, cols, count, tiles, *rest):
    own, other = rest[:PARTS], rest[PARTS : 2 * PARTS]
    outs = rest[2 * PARTS : 2 * PARTS + 4]
    out, flat, held, sems = rest[2 * PARTS + 4 :]
    copies = fetch(tiles, held, sems)
    core = lax.axis_index("core")
    y = lax.axis_index("y")
    here = 2 * lax.axis_index("row") + lax.axis_index("sk")
    slots, tb, _ = held.shape
    depth = tb // PARTS
    out[...] = jnp.zeros_like(out)
    for block, pieces in ((core, own), (1 - core, other)):
        for away, piece in enumerate(pieces):
            part = lax.rem(y - away + PARTS, PARTS)
            here_part = pl.ds(pl.multiple_of(part * depth, depth), depth)
            for h in range(piece.shape[0]):
                flat[block, h * SIDE : (h + 1) * SIDE, here_part] = piece[h].astype(BF16).T
    for s in range(slots):
        for copy in copies[s]:
            copy.wait()

        @pl.when(s < count[0])
        def _():
            prod = dot(flat[rows[s]], held[s], ((1,), (0,)))
            for q in range(2):
                for n in range(tb // 2 // SIDE):
                    at = q * (tb // 2) + n * SIDE
                    out[2 * cols[s] + q, n] += prod[:, at : at + SIDE]

    for n in range(4):
        outs[n][...] = out[here ^ n]


def backward(rows, cols, count, tiles, own, other):
    slots, tb, _ = tiles.shape
    width = own[0].shape[0] * SIDE
    quarter = (tb // 2 // SIDE, width, SIDE)
    return pl.pallas_call(
        backward_kernel,
        in_specs=[SMEM, SMEM, SMEM, ANY] + [VMEM] * (2 * PARTS),
        out_specs=[VMEM] * 4,
        out_shape=[jax.ShapeDtypeStruct(quarter, F32)] * 4,
        scratch_shapes=[
            pltpu.VMEM((4,) + quarter, F32),
            pltpu.VMEM((2, width, tb), BF16),
            pltpu.VMEM(tiles.shape, BF16),
            pltpu.SemaphoreType.DMA((slots, PARTS)),
        ],
        compiler_params=pltpu.CompilerParams(vmem_limit_bytes=48 * MIB),
        name="backward",
    )(rows, cols, count, tiles, *own, *other)


def block_pairs(n):
    return [(i, j) for i in range(n) for j in range(i, n)]


def gram_kernel(*refs):
    low, high, keep, send, zt = refs[-5:]
    core = lax.axis_index("core")
    sk = lax.axis_index("sk")
    parts = refs[0:4]
    chunks, narrow, _ = refs[0].shape
    for far in range(2):
        rows = pl.ds(pl.multiple_of((sk ^ far) * narrow, narrow), narrow)
        for n in range(chunks):
            zt[rows, n * SIDE : (n + 1) * SIDE] = parts[far][n] + parts[far + 2][n]
    low[...] = zt[0:narrow, :]
    high[...] = zt[narrow:, :]
    width = zt.shape[0]
    pairs = block_pairs(width // SIDE)
    half = len(pairs) // 2
    for i in range(width // SIDE):
        lhs = zt[i * SIDE : (i + 1) * SIDE, :]
        prod = dot(lhs, zt[i * SIDE :, :], ((1,), (1,)), HIGH)
        for n, (a, b) in enumerate(pairs):
            if a != i:
                continue
            block = prod[:, (b - i) * SIDE : (b - i + 1) * SIDE]

            @pl.when(core == n // half)
            def _():
                keep[n % half] = block

            @pl.when(core != n // half)
            def _():
                send[n % half] = block


def gram_of(parts):
    chunks, deep, _ = parts[0].shape
    width = 2 * deep
    half = len(block_pairs(width // SIDE)) // 2
    blocks = jax.ShapeDtypeStruct((half, SIDE, SIDE), F32)
    return pl.pallas_call(
        gram_kernel,
        in_specs=[VMEM] * len(parts),
        out_specs=[VMEM] * 4,
        out_shape=[jax.ShapeDtypeStruct((deep, chunks * SIDE), F32)] * 2 + [blocks, blocks],
        scratch_shapes=[pltpu.VMEM((width, chunks * SIDE), F32)],
        compiler_params=pltpu.CompilerParams(vmem_limit_bytes=32 * MIB),
        name="gram",
    )(*parts)


def spread_rows(x, n):
    return jnp.broadcast_to(x[n : n + 1, :], (GROUP, SIDE))


def spread_lanes(x, n):
    return jnp.broadcast_to(x[:, n : n + 1], (GROUP, SIDE))


def eliminate(d, base):
    count = SUB // GROUP
    lanes = d.shape[1] // SIDE
    sub = lax.broadcasted_iota(jnp.int32, (GROUP, SIDE), 0)
    rows = [
        [d[base + GROUP * p : base + GROUP * (p + 1), SIDE * t : SIDE * (t + 1)] for t in range(lanes)]
        for p in range(count)
    ]

    def columns(b):
        first = base + GROUP * b
        return [[spread_lanes(rows[p][0], first + m) for p in range(b, count)] for m in range(GROUP)]

    cols = columns(0)
    for b in range(count):
        ahead = columns(b + 1) if b + 1 < count else []
        scale = jnp.zeros((GROUP, SIDE), F32)
        for m in range(GROUP):
            col = cols[m]
            inv = lax.rsqrt(spread_rows(col[0], m))
            inv2 = inv * inv
            for n in range(m + 1, GROUP):
                mult = spread_rows(col[0], n)
                cols[n] = [c - (l * mult) * inv2 for c, l in zip(cols[n], col)]
            scale = jnp.where(sub == m, inv, scale)
            low = [jnp.where(sub > m, col[0], 0.0) * inv2] + [l * inv2 for l in col[1:]]
            for n in range(len(ahead)):
                mult = spread_rows(col[1], n)
                ahead[n] = [c - l * mult for c, l in zip(ahead[n], low[1:])]
            for t in range(lanes):
                u = spread_rows(rows[b][t], m)
                for p in range(b, count):
                    rows[p][t] = rows[p][t] - low[p - b] * u
        for t in range(lanes):
            rows[b][t] = rows[b][t] * scale
        cols = ahead
    for p in range(count):
        for t in range(lanes):
            d[base + GROUP * p : base + GROUP * (p + 1), SIDE * t : SIDE * (t + 1)] = rows[p][t]


def cholesky_kernel(scale, own, other, upper, inverse, d):
    core = lax.axis_index("core")
    width = upper.shape[0]
    nb = width // SIDE
    pairs = block_pairs(nb)
    half = len(pairs) // 2
    upper[...] = jnp.zeros_like(upper)
    inverse[...] = jnp.zeros_like(inverse)
    for n, (i, j) in enumerate(pairs):
        spot = (slice(i * SIDE, (i + 1) * SIDE), slice(j * SIDE, (j + 1) * SIDE))

        @pl.when(core == n // half)
        def _():
            upper[spot] = own[n % half] * scale

        @pl.when(core != n // half)
        def _():
            upper[spot] = other[n % half] * scale

    row = lax.broadcasted_iota(jnp.int32, (SIDE, SIDE), 0)
    col = lax.broadcasted_iota(jnp.int32, (SIDE, SIDE), 1)
    eye = (row == col).astype(F32)

    def step(k, carry):
        here = pl.ds(pl.multiple_of(k * SIDE, SIDE), SIDE)
        d[:, 0:SIDE] = upper[here, here]
        d[:, SIDE:] = eye
        for s in range(SIDE // SUB):
            base = s * SUB
            eliminate(d, base)
            if base + SUB < SIDE:
                panel = d[base : base + SUB, :]
                for r in (slice(base + SUB, base + 2 * SUB), slice(base + 2 * SUB, SIDE)):
                    if r.start < r.stop:
                        d[r, :] -= dot(panel[:, r], panel, ((0,), (0,)), HIGH)
        upper[here, here] = jnp.where(row <= col, d[:, 0:SIDE], 0.0)
        inverse[here, here] = jnp.where(row >= col, d[:, SIDE:], 0.0)

        for kk in range(nb):

            @pl.when(k == kk)
            def _():
                lo, hi = kk * SIDE, (kk + 1) * SIDE
                w = inverse[lo:hi, lo:hi]
                if hi < width:
                    upper[lo:hi, hi:] = dot(w, upper[lo:hi, hi:], ((1,), (0,)), HIGH)
                if lo > 0:
                    inverse[lo:hi, 0:lo] = dot(w, inverse[lo:hi, 0:lo], ((1,), (0,)), HIGH)
                if hi < width:
                    left = upper[lo:hi, hi:].T
                    prod = dot(left, upper[lo:hi, hi:], ((1,), (0,)), HIGH)
                    for i in range(kk + 1, nb):
                        r = slice(i * SIDE, (i + 1) * SIDE)
                        o = slice((i - kk - 1) * SIDE, (i - kk) * SIDE)
                        upper[r, i * SIDE :] -= prod[o, (i - kk - 1) * SIDE :]
                    inverse[hi:, 0:hi] -= dot(left, inverse[lo:hi, 0:hi], ((1,), (0,)), HIGH)

        return carry

    lax.fori_loop(0, nb, step, 0)


def cholesky(own, other, total_rows, width):
    square = jax.ShapeDtypeStruct((width, width), F32)
    return pl.pallas_call(
        functools.partial(cholesky_kernel, 1.0 / total_rows),
        out_shape=[square, square],
        scratch_shapes=[pltpu.VMEM((SIDE, 2 * SIDE), F32)],
        compiler_params=pltpu.CompilerParams(vmem_limit_bytes=24 * MIB),
        cost_estimate=pl.CostEstimate(flops=2**34, bytes_accessed=2**22, transcendentals=0),
        name="cholesky",
    )(own, other)


def split(x):
    high = x.astype(BF16)
    return high, (x - high.astype(F32)).astype(BF16)


def basis_kernel(inverse, *refs):
    lows = [refs[0:1], refs[1:2], refs[2:4], refs[4:5]]
    highs = refs[5:9]
    out, done, store = refs[9:]
    here = 2 * lax.axis_index("row") + lax.axis_index("sk")
    chunk, narrow = done.shape[1:]
    form = ((1,), (0,))
    rows = pl.ds(pl.multiple_of(lax.axis_index("sk") * narrow, narrow), narrow)
    weights = [split(inverse[rows, k * narrow : (k + 1) * narrow]) for k in range(2)]
    stores = []
    for n in range(4):
        total = 0.0
        parts = (jnp.concatenate([ref[...] for ref in lows[n]], axis=0), highs[n][...])
        for (w_high, w_low), part in zip(weights, parts):
            high, low = split(part)
            total += dot(w_high, high, form) + (dot(w_high, low, form) + dot(w_low, high, form))
        done[n] = total.T
        place = pl.ds(pl.multiple_of((here ^ n) * chunk, chunk), chunk)
        stores.append(pltpu.make_async_copy(done.at[n], out.at[place, :], store.at[n]))
        stores[n].start()
    for copy in stores:
        copy.wait()


def basis_of(inverse, lows, highs):
    narrow, chunk = lows[0].shape
    return pl.pallas_call(
        basis_kernel,
        in_specs=[VMEM] * 10,
        out_specs=ANY,
        out_shape=jax.ShapeDtypeStruct((4 * chunk, narrow), F32),
        scratch_shapes=[pltpu.VMEM((4, chunk, narrow), F32), pltpu.SemaphoreType.DMA((4,))],
        compiler_params=pltpu.CompilerParams(vmem_limit_bytes=32 * MIB),
        name="basis",
    )(inverse, *lows, *highs)


def swap(x):
    return lax.ppermute(x, "core", [(0, 1), (1, 0)])


def shift(x, axes, n):
    size = lax.axis_size(axes)
    return lax.ppermute(x, axes, [(i, (i + n) % size) for i in range(size)])


def across(x, n, to=range(4)):
    return lax.ppermute(x, RING, [(i ^ n, i) for i in to])


def exchange(x, axes):
    return lax.all_to_all(x, axes, 0, 0, tiled=True)


def spread(x, axes):
    n = lax.axis_size(axes)
    return exchange(jnp.broadcast_to(x[None], (n,) + x.shape), axes)


def on_device(tiles, tile_rows, tile_cols, tile_count, sketch):
    blocks = tiles[0, 0]
    rows = tile_rows[0, 0]
    cols = tile_cols[0, 0]
    count = tile_count[0]
    tb = blocks.shape[1]
    narrow = sketch.shape[1]
    width = narrow * lax.axis_size("sk")
    total_rows = sketch.shape[0] * lax.axis_size(("z", "y", "core"))

    keep, send = forward(rows, cols, count, blocks, sketch.reshape(-1, tb, narrow))
    received = swap(send)
    pieces = [keep[n] + received[n] for n in range(PARTS)]
    for n in (1, 3, 2):
        pieces[n] = shift(pieces[n], "y", n)
    part = pieces[0] + pieces[1] + pieces[3] + pieces[2]
    deep = lax.axis_size("z")
    pieces = exchange(part.reshape(deep, -1, SIDE), "z")
    piece = jnp.sum(pieces, axis=0) * 0.75
    part = spread(piece, "z").reshape(part.shape)
    own = [part] + [shift(part, "y", n) for n in range(1, PARTS)]
    other = [swap(p) for p in own]
    pieces = backward(rows, cols, count, blocks, own, other)
    moved = [pieces[0]] + [across(pieces[n], n) for n in range(1, 4)]
    low, high, keep, send = gram_of(moved)

    lows = [low, across(low, 1), None, across(low, 3)]
    half = keep + swap(send)
    sheet = lax.axis_size(SHEET)
    pieces = exchange(half.reshape(sheet, -1, SIDE), SHEET)
    piece, lows[1], lows[3] = lax.optimization_barrier((jnp.sum(pieces, axis=0), lows[1], lows[3]))
    late, _ = lax.optimization_barrier((high, piece))
    highs = [high, across(late, 1, ODD), None, across(late, 3, ODD)]
    piece = jnp.sum(spread(piece, "z"), axis=0)
    piece, highs[1], highs[3] = lax.optimization_barrier((piece, highs[1], highs[3]))
    own_g = spread(piece, SHEET).reshape(keep.shape)
    first, second, late, _ = lax.optimization_barrier((lows[3], lows[1], high, own_g))
    middle = narrow // 2
    relayed = [across(first[:middle], 1), across(second[middle:], 3)]
    lows[2] = None
    highs[2] = across(late, 2, ODD)
    other_g = swap(own_g)

    upper, inverse = cholesky(own_g, other_g, total_rows, width)
    return basis_of(inverse, lows[:2] + relayed + lows[3:], highs), upper


def solution(mesh):
    fine = Mesh(mesh.devices.reshape(2, 8, 4, 2, 2), ("row", "z", "y", "core", "sk"))
    col = ("z", "y", "core")
    return jax.shard_map(
        on_device,
        mesh=fine,
        in_specs=(
            P("row", col, None, None, None),
            P("row", col, None),
            P("row", col, None),
            P("row", col),
            P(col, "sk"),
        ),
        out_specs=(P(col, "sk"), P()),
        check_vma=False,
    )
```
